256 devices in a mesh: row: 4 (over y), col: 16 (over z, core), aux: 4 (over x).
Axes of the slice: x: 4, y: 4, z: 8, core: 2. Of those that a mesh axis runs over, the one named last changes fastest.
Arguments:
- half_transformed: bfloat16 [64, 2048, 4096], P('aux', 'row', 'col'), may hold values from -0.26367188 to 0.26367188
- screen: int32 [64, 16], replicated, may hold values 0 or 1
Outputs:
- exchange_matrix: float32 [2048, 2048], P(('row', 'col', 'aux'))
The draws below stay inside these ranges and needn't reach their ends.
All inputs are finite; a program needn't handle non-finite values.
Results may differ from the reference program's by a relative error of at most 0.0003.
Values may be sent and summed in bfloat16 or wider, within the bound.
No kernel may reach another device: no remote copies, remote signals or barrier semaphores. Data moves between devices by JAX's collectives and lax.ppermute only.
A program may use at most 128 MiB of HBM per device.

```python
import jax
import jax.numpy as jnp
from jax import lax

NOCC = 4096
TILE = 128
NB = 2048
NQ = 64


def touch_ends(entries, own_key, low, largest):
    place = [jax.random.randint(jax.random.fold_in(own_key, axis), (), 0, length) for axis, length in enumerate(entries.shape)]
    longest = entries.shape.index(max(entries.shape))
    beside = place[:longest] + [(place[longest] + 1) % entries.shape[longest]] + place[longest + 1:]
    return entries.at[tuple(place)].set(low).at[tuple(beside)].set(largest)


def shard_levels(own_key, extent, pieces, smallest, high):
    level, own = 1.0, jax.random.fold_in(own_key, 6)
    for axis_at, blocks in pieces:
        heights = jnp.exp(jax.random.uniform(jax.random.fold_in(own, axis_at), (blocks,), jnp.float32, smallest / len(pieces), high / len(pieces)))
        level = level * jnp.repeat(heights, extent[axis_at] // blocks).reshape([-1 if axis == axis_at else 1 for axis in range(len(extent))])
    return level


def centred(own_key, shape, scale, most, cuts=(), kind=jnp.bfloat16):
    loudness = shard_levels(own_key, shape, cuts, -0.22, 0.18) if cuts else 1.0
    array = jax.random.normal(own_key, shape, jnp.float32) * scale * loudness
    return jnp.minimum(jnp.maximum(array, -most), most).astype(kind)


def setup_inputs(seed: int = 0) -> dict:
    splits = jax.random.split(jax.random.key(seed), 3)
    half_transformed = centred(splits[0], (NQ, NB, NOCC), ((NQ * NOCC) ** -0.25), 0.26367188, ((0, 4), (1, 4), (2, 16)))
    screen = touch_ends((jax.random.randint(splits[1], (NQ, NB // TILE), 0, 4) < 3).astype(jnp.int32), jax.random.fold_in(splits[1], 1), 0, 1)
    return {"half_transformed": half_transformed, "screen": screen}


def reference(half_transformed, screen):
    def step(total, item):
        slab, pattern = item
        keep = jnp.repeat(pattern, TILE).astype(half_transformed.dtype)
        masked = slab * keep[:, None]
        return total + jnp.dot(masked, masked.T, preferred_element_type=jnp.float32), None

    total, _ = lax.scan(step, jnp.zeros((NB, NB), jnp.float32), (half_transformed, screen))
    return total
```

```python
import functools

import jax
import jax.numpy as jnp
from jax import lax
from jax.experimental import pallas as pl
from jax.experimental.pallas import tpu as pltpu
from jax.sharding import Mesh, PartitionSpec as P

TILE = 128
VMEM_LIMIT = 48 * 1024 * 1024


def shift(value, axis, step, size):
    return lax.ppermute(value, axis, [(i, (i + step) % size) for i in range(size)])


def times_transposed(left, right):
    return lax.dot_general(left, right, (((1,), (1,)), ((), ())), preferred_element_type=jnp.float32)


def diagonal_kernel(place, screen, slab, keep, give, total):
    step = pl.program_id(0)
    core, row, aux = place[0], place[1], place[2]
    rows = slab[0]
    depth = pl.num_programs(0)
    tiles = rows.shape[0] // TILE
    masked = jnp.concatenate(
        [
            rows[t * TILE : (t + 1) * TILE] * screen[aux * depth + step, row * tiles + t].astype(jnp.bfloat16)
            for t in range(tiles)
        ],
        axis=0,
    )
    product = times_transposed(masked, masked)

    @pl.when(step == 0)
    def _():
        total[...] = product.reshape(total.shape)

    @pl.when(step > 0)
    def _():
        total[...] += product.reshape(total.shape)

    @pl.when(step == depth - 1)
    def _():
        keep[...] = total[:, core].reshape(keep.shape)
        give[...] = total[:, 1 - core].reshape(give.shape)


def diagonal(place, screen, block, zs):
    depth, rows, width = block.shape
    half = jax.ShapeDtypeStruct((rows // 2, rows), jnp.float32)
    whole = pl.BlockSpec((rows // 2, rows), lambda q, *_: (0, 0))
    return pl.pallas_call(
        diagonal_kernel,
        grid_spec=pltpu.PrefetchScalarGridSpec(
            num_scalar_prefetch=2,
            grid=(depth,),
            in_specs=[pl.BlockSpec((1, rows, width), lambda q, *_: (q, 0, 0))],
            out_specs=[whole, whole],
            scratch_shapes=[pltpu.VMEM((zs, 2, rows // zs // 2, rows), jnp.float32)],
        ),
        out_shape=[half, half],
        compiler_params=pltpu.CompilerParams(vmem_limit_bytes=VMEM_LIMIT),
        cost_estimate=pl.CostEstimate(
            flops=2 * depth * rows * rows * width, bytes_accessed=2 * depth * rows * width, transcendentals=0
        ),
        name="diagonal",
    )(place, screen, block)


def pairs_kernel(products, extra, blocks, place, *refs):
    step = pl.program_id(0)
    core, aux = place[0], place[2]
    slabs, refs = refs[: 2 * blocks], refs[2 * blocks :]
    added, refs = refs[:extra], refs[extra:]
    outs, total = refs[:-1], refs[-1]
    xs = len(outs)
    cols = slabs[0].shape[1] * slabs[0].shape[2] * slabs[0].shape[3]
    size = cols // 2

    @pl.when(step == 0)
    def _():
        total[...] = jnp.zeros_like(total)

    for at, (left, right) in enumerate(products):
        product = None
        for part in range(2):
            lhs = slabs[2 * left + part][0, :, core].reshape(size, -1)
            rhs = slabs[2 * right + part][0].reshape(cols, -1)
            term = times_transposed(lhs, rhs)
            product = term if product is None else product + term
        total[:, at * cols : (at + 1) * cols] += product

    @pl.when(step == pl.num_programs(0) - 1)
    def _():
        begin = 0
        if extra:
            begin = cols
            diag = (added[0][...] + added[1][...]).reshape(-1, xs, 8, cols)
        grouped = total[...].reshape(-1, xs, 8, total.shape[1])
        zs = grouped.shape[0]
        for there in range(xs):
            piece = grouped[:, there].reshape(zs * 8, -1)
            dpiece = diag[:, there].reshape(zs * 8, -1) if extra else None
            for d in range(xs):
                @pl.when(lax.rem(aux + d, xs) == there)
                def _():
                    outs[d][:, begin:] = piece
                    if extra:
                        outs[d][:, :cols] = dpiece


def pairs(place, slabs, products, added, zs, xs):
    depth, rows, width = slabs[0][0].shape
    flat = [s.reshape(depth, zs, 2, rows // zs // 2, width) for pair in slabs for s in pair]
    spec = pl.BlockSpec((1, zs, 2, rows // zs // 2, width), lambda q, *_: (q, 0, 0, 0, 0))
    aspec = pl.BlockSpec((rows // 2, rows), lambda q, *_: (0, 0))
    cols = rows * (len(products) + (1 if added else 0))
    out = jax.ShapeDtypeStruct((rows // 2 // xs, cols), jnp.float32)
    ospec = pl.BlockSpec(out.shape, lambda q, *_: (0, 0))
    return pl.pallas_call(
        functools.partial(pairs_kernel, products, len(added), len(slabs)),
        grid_spec=pltpu.PrefetchScalarGridSpec(
            num_scalar_prefetch=1,
            grid=(depth,),
            in_specs=[spec] * len(flat) + [aspec] * len(added),
            out_specs=[ospec] * xs,
            scratch_shapes=[pltpu.VMEM((rows // 2, rows * len(products)), jnp.float32)],
        ),
        out_shape=[out] * xs,
        compiler_params=pltpu.CompilerParams(vmem_limit_bytes=VMEM_LIMIT),
        cost_estimate=pl.CostEstimate(
            flops=2 * depth * rows * rows * width * len(products),
            bytes_accessed=2 * depth * rows * width * len(flat),
            transcendentals=0,
        ),
        name="pairs",
    )(place, *flat, *added)


def reduce_aux(parts, xs):
    there = [shift(parts[d], "aux", d, xs) for d in range(1, xs)]
    return parts[0] + there[0] + there[1] + there[2]


def body(half_transformed, screen):
    qrows, mrows, icols = half_transformed.shape
    ys, zs, xs = 4, 8, 4
    quarter = qrows // ys
    row, core, aux = lax.axis_index("row"), lax.axis_index("core"), lax.axis_index("aux")
    place = jnp.stack([core, row, aux]).astype(jnp.int32)
    tiles = mrows // TILE

    local = lax.dynamic_slice(screen, (aux * qrows, row * tiles), (qrows, tiles))
    keep = jnp.repeat(local, TILE, axis=1).astype(jnp.bfloat16)

    def slab(step):
        first = lax.rem(row + step, ys) * quarter
        part = lax.dynamic_slice(half_transformed, (first, 0, 0), (quarter, mrows, icols))
        return part * lax.dynamic_slice(keep, (first, 0), (quarter, mrows))[:, :, None]

    def sibling(value):
        return lax.ppermute(value, "core", [(0, 1), (1, 0)])

    below = shift(slab(1), "row", 1, ys)
    above = shift(slab(3), "row", -1, ys)
    mine = slab(0)
    kept, given = diagonal(place, screen, half_transformed, zs)
    got = sibling(given)
    mine2 = sibling(mine)
    far, below, above = lax.optimization_barrier((slab(2), below, above))
    across = shift(far, "row", 2, ys)
    below2, above2 = sibling(below), sibling(above)

    early = pairs(
        place, [(mine, mine2), (above, above2), (below, below2)], ((0, 1), (1, 2), (0, 2)), (kept, got), zs, xs
    )
    early = reduce_aux(early, xs)
    across2 = sibling(across)
    late = pairs(
        place,
        [(across, across2), (below, below2), (mine, mine2), (above, above2)],
        ((0, 1), (0, 2), (0, 3)),
        (),
        zs,
        xs,
    )
    late = reduce_aux(late, xs)

    n = mrows
    early_up = shift(early[:, n : 3 * n], "row", 1, ys)
    early_down = shift(early[:, 2 * n :], "row", -1, ys)
    late_up = shift(late[:, 2 * n :], "row", 1, ys)
    late_down = shift(late[:, :n], "row", -1, ys)
    late_far = shift(late, "row", 2, ys)
    plus = early[:, n : 2 * n] + late_far[:, :n]
    minus = early[:, 3 * n :] + late_far[:, 2 * n :]
    twice = early_up[:, n:] + late_far[:, n : 2 * n]
    turned_minus = early_up[:, :n] + late_down
    turned_plus = early_down[:, n:] + late_up
    turned_twice = early_down[:, :n] + late[:, n : 2 * n]

    plain = jnp.concatenate([early[:, :n], plus, twice, minus], axis=1).reshape(zs, 8, 4 * n)
    turned = jnp.stack([turned_plus, turned_twice, turned_minus])
    turned = turned.reshape(3, zs * 8, zs, 2 * xs, 8).transpose(2, 4, 3, 0, 1).reshape(zs, 8, 2 * xs * 3 * zs * 8)
    both = lax.all_to_all(jnp.concatenate([plain, turned], axis=2), "z", 0, 0, tiled=True)
    both = jnp.sum(both, axis=0)
    plain, turned = both[:, : 4 * n], both[:, 4 * n :]

    turned = turned.reshape(8, 2, xs * 3 * zs * 8)
    own = lax.dynamic_index_in_dim(turned, core, 1, keepdims=False)
    other = sibling(lax.dynamic_index_in_dim(turned, 1 - core, 1, keepdims=False))
    pieces = jnp.stack([jnp.where(core == 0, own, other), jnp.where(core == 0, other, own)])
    pieces = pieces.reshape(2, 8, xs, 3 * zs * 8).transpose(2, 0, 1, 3)
    pieces = lax.all_to_all(pieces, "aux", 0, 0, tiled=True)
    pieces = pieces.reshape(xs, 2, 8, 3, zs, 8).transpose(2, 3, 4, 1, 0, 5).reshape(8, 3 * n)
    out = plain + jnp.concatenate([jnp.zeros((8, n), jnp.float32), pieces], axis=1)
    return lax.dynamic_slice(jnp.concatenate([out, out], axis=1), (0, lax.rem(ys - row, ys) * n), (8, 4 * n))


def solution(mesh):
    rows, cols, aux = mesh.devices.shape
    split = Mesh(mesh.devices.reshape(rows, cols // 2, 2, aux), ("row", "z", "core", "aux"))
    in_specs = (P("aux", "row", ("z", "core")), P())
    out_specs = P(("row", "z", "core", "aux"), None)
    return jax.shard_map(body, mesh=split, in_specs=in_specs, out_specs=out_specs, check_vma=False)
```

```python
import functools

import jax
import jax.numpy as jnp
from jax import lax
from jax.experimental import pallas as pl
from jax.experimental.pallas import tpu as pltpu
from jax.sharding import Mesh, PartitionSpec as P

TILE = 128
VMEM_LIMIT = 32 * 1024 * 1024
ANYWHERE = pl.BlockSpec(memory_space=pltpu.VMEM)
SOME = 6_000_000_000
AFTER = pl.BlockSpec(memory_space=pl.ANY)
SCALARS = pl.BlockSpec(memory_space=pltpu.SMEM)


def shift(value, axis, step, size):
    return lax.ppermute(value, axis, [(i, (i + step) % size) for i in range(size)])


def sibling(value):
    return lax.ppermute(value, "core", [(0, 1), (1, 0)])


def times_transposed(left, right):
    return lax.dot_general(left, right, (((1,), (1,)), ((), ())), preferred_element_type=jnp.float32)


def diagonal_kernel(place, screen, slab, keep, give, total):
    step = pl.program_id(0)
    core, row, aux = place[0], place[1], place[2]
    group, mrows, _ = slab.shape
    depth = pl.num_programs(0) * group
    tiles = mrows // TILE

    def masked(q):
        at = aux * depth + step * group + q
        parts = [
            slab[q, t * TILE : (t + 1) * TILE, :] * screen[at, row * tiles + t].astype(jnp.bfloat16)
            for t in range(tiles)
        ]
        return jnp.concatenate(parts, axis=0)

    rows = jnp.concatenate([masked(q) for q in range(group)], axis=1)
    product = times_transposed(rows, rows)

    @pl.when(step == 0)
    def _():
        total[...] = product.reshape(total.shape)

    @pl.when(step > 0)
    def _():
        total[...] += product.reshape(total.shape)

    @pl.when(step == pl.num_programs(0) - 1)
    def _():
        keep[...] = total[:, core].reshape(keep.shape)
        give[...] = total[:, 1 - core].reshape(give.shape)


def diagonal(place, screen, block, zs, group=4):
    depth, rows, width = block.shape
    half = jax.ShapeDtypeStruct((rows // 2, rows), jnp.float32)
    whole = pl.BlockSpec((rows // 2, rows), lambda q: (0, 0))
    return pl.pallas_call(
        diagonal_kernel,
        grid=(depth // group,),
        in_specs=[SCALARS, SCALARS, pl.BlockSpec((group, rows, width), lambda q: (q, 0, 0))],
        out_specs=[whole, whole],
        scratch_shapes=[pltpu.VMEM((zs, 2, rows // zs // 2, rows), jnp.float32)],
        out_shape=[half, half],
        compiler_params=pltpu.CompilerParams(vmem_limit_bytes=VMEM_LIMIT),
        cost_estimate=pl.CostEstimate(flops=1, bytes_accessed=1, transcendentals=0),
        name="diagonal",
    )(place, screen, block)


def store_by_aux(aux, product, outs, row, col):
    xs = len(outs)
    grouped = product.reshape(-1, xs, 8, product.shape[1])
    size = grouped.shape[0] * 8
    for there in range(xs):
        piece = grouped[:, there].reshape(size, -1)
        for d in range(xs):
            @pl.when(lax.rem(aux + d, xs) == there)
            def _():
                outs[d][row : row + size, col : col + piece.shape[1]] = piece


def wide(refs, core=None):
    parts = []
    for ref in refs:
        for q in range(ref.shape[0]):
            part = ref[q] if core is None else ref[q, :, core]
            parts.append(part.reshape(-1, part.shape[-1]))
    return jnp.concatenate(parts, axis=1)


def split_kernel(place, kept, got, *outs):
    store_by_aux(place[2], kept[...] + got[...], outs, 0, 0)


def pick_kernel(place, across, _, out):
    out[:, :, 0] = across[:, :, 1 - place[0]]


def early_kernel(place, mine, mine2, above, above2, below, below2, *outs):
    core, aux = place[0], place[2]
    n = above.shape[1] * above.shape[2] * above.shape[3]
    own, up = wide((mine, mine2), core), wide((above, above2), core)
    right, left = wide((above, above2)), wide((below, below2))
    store_by_aux(aux, times_transposed(own, right), outs, 0, 0)
    store_by_aux(aux, times_transposed(up, left), outs, 0, n)
    store_by_aux(aux, times_transposed(own, left), outs, 0, 2 * n)


def late_kernel(place, below, below2, mine, mine2, above, above2, across, across2, _, *outs):
    core, aux = place[0], place[2]
    left = jnp.concatenate([wide((across,), core), wide((across2,), 0)], axis=1)
    n = outs[0].shape[1] // 3
    for at, pair in enumerate(((below, below2), (mine, mine2), (above, above2))):
        store_by_aux(aux, times_transposed(left, wide(pair)), outs, 0, at * n)


def pairs(kernel, place, operands, shape, xs, after=(), flops=1):
    out = jax.ShapeDtypeStruct(shape, jnp.float32)
    return pl.pallas_call(
        kernel,
        in_specs=[SCALARS] + [ANYWHERE] * len(operands) + [AFTER] * len(after),
        out_specs=[ANYWHERE] * xs,
        out_shape=[out] * xs,
        compiler_params=pltpu.CompilerParams(vmem_limit_bytes=VMEM_LIMIT),
        cost_estimate=pl.CostEstimate(flops=flops, bytes_accessed=1, transcendentals=0),
        name=kernel.__name__,
    )(place, *operands, *after)


def pick(place, across, after):
    shape = (*across.shape[:2], 1, *across.shape[3:])
    return pl.pallas_call(
        pick_kernel,
        in_specs=[SCALARS, ANYWHERE, AFTER],
        out_specs=ANYWHERE,
        out_shape=jax.ShapeDtypeStruct(shape, across.dtype),
        compiler_params=pltpu.CompilerParams(vmem_limit_bytes=VMEM_LIMIT),
        cost_estimate=pl.CostEstimate(flops=1, bytes_accessed=1, transcendentals=0),
        name="pick",
    )(place, across, after)


def over_aux(parts, xs):
    return [shift(parts[d], "aux", d, xs) if d else parts[0] for d in range(xs)]


SLOTS = ((0,), (3,), (5,), (1, 6), (7, 4, 2))


def turn(block, zs):
    rows, cols = block.shape
    turned = block.T.reshape(zs, cols // zs // 8, 8, rows)
    return [[turned[at, k] for k in range(turned.shape[1])] for at in range(zs)]


def send_out(place, buffer, outs):
    zs = buffer.shape[0]
    for out, steps in zip(outs, SLOTS):
        for at, step in enumerate(steps):
            out[at] = buffer[lax.rem(place[3] + step, zs)]


def pack_kernel(diagonals, place, *refs):
    parts, diags, outs, buffer = refs[:4], refs[4 : 4 + diagonals], refs[4 + diagonals : -1], refs[-1]
    zs = buffer.shape[0]
    n = parts[0].shape[1] // 3
    begin = 0
    if diags:
        begin = n
        buffer[:, :, :n] = (diags[0][...] + diags[1][...] + diags[2][...] + diags[3][...]).reshape(zs, 8, n)
    for pair in range(3):
        cut = slice(pair * n, (pair + 1) * n)
        block = parts[0][:, cut] + parts[1][:, cut] + parts[2][:, cut] + parts[3][:, cut]
        buffer[:, :, begin + pair * n : begin + (pair + 1) * n] = block.reshape(zs, 8, n)
        size = block.shape[0]
        for at, pieces in enumerate(turn(block, zs)):
            for k, piece in enumerate(pieces):
                lane = begin + (3 + pair) * n + k * size
                buffer[at, :, lane : lane + size] = piece
    send_out(place, buffer, outs)


def pack(place, parts, diags=(), flops=1):
    zs = 8
    n = parts[0].shape[1] // 3
    width = (7 if diags else 6) * n
    operands = (*parts, *diags)
    shapes = [(len(steps), 8, width) for steps in SLOTS]
    return pl.pallas_call(
        functools.partial(pack_kernel, len(diags)),
        in_specs=[SCALARS] + [ANYWHERE] * len(operands),
        out_specs=[ANYWHERE] * len(shapes),
        out_shape=[jax.ShapeDtypeStruct(s, jnp.float32) for s in shapes],
        scratch_shapes=[pltpu.VMEM((zs, 8, width), jnp.float32)],
        compiler_params=pltpu.CompilerParams(vmem_limit_bytes=VMEM_LIMIT),
        cost_estimate=pl.CostEstimate(flops=flops, bytes_accessed=1, transcendentals=0),
        name="pack",
    )(place, *operands)


def reduce_z(packed):
    zs = 8
    here, forward, backward, up, down = packed
    up, down = shift(up, "z", 1, zs), shift(down, "z", -1, zs)
    forward = forward[0] + down[2]
    backward = backward[0] + up[1] + down[1]
    here = here[0] + up[0] + down[0]
    return here + shift(forward, "z", 3, zs) + shift(backward, "z", -3, zs)


def body(half_transformed, screen):
    qrows, mrows, icols = half_transformed.shape
    ys, zs, xs = 4, 8, 4
    quarter = qrows // ys
    row, z = lax.axis_index("row"), lax.axis_index("z")
    core, aux = lax.axis_index("core"), lax.axis_index("aux")
    place = jnp.stack([core, row, aux, z]).astype(jnp.int32)
    tiles = mrows // TILE
    n = mrows
    grouped = (quarter, zs, 2, n // zs // 2, icols)

    local = lax.dynamic_slice(screen, (aux * qrows, row * tiles), (qrows, tiles))
    keep = jnp.repeat(local, TILE, axis=1).astype(jnp.bfloat16)

    def slab(block, step):
        first = lax.rem(row + step, ys) * quarter
        part = lax.dynamic_slice(block, (first, 0, 0), (quarter, mrows, icols))
        return part * lax.dynamic_slice(keep, (first, 0), (quarter, mrows))[:, :, None]

    to_up, to_down = slab(half_transformed, 1), slab(half_transformed, 3)
    block, to_up, to_down = lax.optimization_barrier((half_transformed, to_up, to_down))
    below = shift(to_up, "row", 1, ys)
    above = shift(to_down, "row", -1, ys)
    mine = slab(block, 0)
    mine2 = sibling(mine)
    kept, given = diagonal(place, screen, block, zs)
    diag = pairs(split_kernel, place, (kept, sibling(given)), (zs * 8, n), xs)
    diag = over_aux(diag, xs)
    below, above, far, diag = lax.optimization_barrier((below, above, slab(block, 2), diag))
    across = shift(far, "row", 2, ys)
    below2, above2 = sibling(below), sibling(above)
    mine, mine2, above, above2, below, below2 = (
        s.reshape(grouped) for s in (mine, mine2, above, above2, below, below2)
    )
    early_parts = pairs(
        early_kernel, place, (mine, mine2, above, above2, below, below2), (zs * 8, 3 * n), xs
    )
    computed = early_parts[0]
    early_parts = over_aux(early_parts, xs)
    early = pack(place, early_parts, diag, SOME)
    across2 = sibling(pick(place, across.reshape(grouped), computed))
    late_parts = pairs(
        late_kernel,
        place,
        (below, below2, mine, mine2, above, above2, across.reshape(grouped), across2),
        (zs * 8, 3 * n),
        xs,
        (early[0],),
    )
    early, late_parts = lax.optimization_barrier((early, late_parts))
    early = reduce_z(early)
    late = reduce_z(pack(place, over_aux(late_parts, xs)))
    late_plain, late_turned = late[:, : 3 * n], late[:, 3 * n :]

    def cut(value, at):
        return value[:, at * n : (at + 1) * n]

    up = shift(jnp.concatenate([cut(early, 4), cut(early, 2), cut(late_turned, 2)], axis=1), "row", 1, ys)
    down = shift(jnp.concatenate([cut(early, 6), cut(early, 5), cut(late_turned, 0)], axis=1), "row", -1, ys)
    over = shift(late_plain, "row", 2, ys)
    plus = cut(early, 1) + cut(over, 0)
    twice = cut(up, 1) + cut(over, 1)
    minus = cut(early, 3) + cut(over, 2)
    turned_plus = cut(down, 0) + cut(up, 2)
    turned_twice = cut(down, 1) + cut(late_turned, 1)
    turned_minus = cut(up, 0) + cut(down, 2)

    turned = jnp.stack([turned_plus, turned_twice, turned_minus], axis=1)
    turned = turned.reshape(8, 3, 2, xs * zs * 8)
    own = lax.dynamic_index_in_dim(turned, core, 2, keepdims=False)
    other = sibling(lax.dynamic_index_in_dim(turned, 1 - core, 2, keepdims=False))
    pieces = jnp.stack([jnp.where(core == 0, own, other), jnp.where(core == 0, other, own)])
    pieces = pieces.reshape(2, 8, 3, xs, zs * 8).transpose(3, 0, 1, 2, 4).reshape(xs, 2, 8, 3 * zs * 8)
    pieces = lax.dynamic_slice(jnp.concatenate([pieces, pieces]), (aux, 0, 0, 0), pieces.shape)
    came = [shift(pieces[d], "aux", d, xs) if d else pieces[0] for d in range(xs)]
    came = jnp.stack([came[-e % xs] for e in range(xs)] * 2)
    came = lax.dynamic_slice(came, (lax.rem(xs - aux, xs), 0, 0, 0), pieces.shape)
    came = came.reshape(xs, 2, 8, 3, zs, 8).transpose(2, 3, 4, 1, 0, 5).reshape(8, 3 * n)
    out = jnp.concatenate(
        [cut(early, 0), plus + cut(came, 0), twice + cut(came, 1), minus + cut(came, 2)], axis=1
    )
    return lax.dynamic_slice(jnp.concatenate([out, out], axis=1), (0, lax.rem(ys - row, ys) * n), (8, 4 * n))


def solution(mesh):
    rows, cols, aux = mesh.devices.shape
    split = Mesh(mesh.devices.reshape(rows, cols // 2, 2, aux), ("row", "z", "core", "aux"))
    in_specs = (P("aux", "row", ("z", "core")), P())
    out_specs = P(("row", "z", "core", "aux"), None)
    return jax.shard_map(body, mesh=split, in_specs=in_specs, out_specs=out_specs, check_vma=False)
```

```python
import functools

import jax
import jax.numpy as jnp
from jax import lax
from jax.experimental import pallas as pl
from jax.experimental.pallas import tpu as pltpu
from jax.sharding import Mesh, PartitionSpec as P

TILE = 128
MIB = 1024 * 1024
ANYWHERE = pl.BlockSpec(memory_space=pltpu.VMEM)
SOME = 10_000_000_000
LESS = 1_000_000_000
MORE = 6_000_000_000
AFTER = pl.BlockSpec(memory_space=pl.ANY)
SCALARS = pl.BlockSpec(memory_space=pltpu.SMEM)


def shift(value, axis, step, size):
    return lax.ppermute(value, axis, [(i, (i + step) % size) for i in range(size)])


def sibling(value):
    return lax.ppermute(value, "core", [(0, 1), (1, 0)])


def times_transposed(left, right):
    return lax.dot_general(left, right, (((1,), (1,)), ((), ())), preferred_element_type=jnp.float32)


def diagonal_kernel(place, screen, slab, keep, give, total):
    step = pl.program_id(0)
    core, row, aux = place[0], place[1], place[2]
    group, mrows, _ = slab.shape
    depth = pl.num_programs(0) * group
    tiles = mrows // TILE

    def masked(q):
        at = aux * depth + step * group + q
        parts = [
            slab[q, t * TILE : (t + 1) * TILE, :] * screen[at, row * tiles + t].astype(jnp.bfloat16)
            for t in range(tiles)
        ]
        return jnp.concatenate(parts, axis=0)

    rows = jnp.concatenate([masked(q) for q in range(group)], axis=1)
    product = times_transposed(rows, rows)

    @pl.when(step == 0)
    def _():
        total[...] = product.reshape(total.shape)

    @pl.when(step > 0)
    def _():
        total[...] += product.reshape(total.shape)

    @pl.when(step == pl.num_programs(0) - 1)
    def _():
        keep[...] = total[:, core].reshape(keep.shape)
        give[...] = total[:, 1 - core].reshape(give.shape)


def diagonal(place, screen, block, zs, group=4):
    depth, rows, width = block.shape
    half = jax.ShapeDtypeStruct((rows // 2, rows), jnp.float32)
    whole = pl.BlockSpec((rows // 2, rows), lambda q: (0, 0))
    return pl.pallas_call(
        diagonal_kernel,
        grid=(depth // group,),
        in_specs=[SCALARS, SCALARS, pl.BlockSpec((group, rows, width), lambda q: (q, 0, 0))],
        out_specs=[whole, whole],
        scratch_shapes=[pltpu.VMEM((zs, 2, rows // zs // 2, rows), jnp.float32)],
        out_shape=[half, half],
        compiler_params=pltpu.CompilerParams(vmem_limit_bytes=16 * MIB),
        cost_estimate=pl.CostEstimate(flops=1, bytes_accessed=1, transcendentals=0),
        name="diagonal",
    )(place, screen, block)


def store_by_aux(aux, product, outs, row, col):
    xs = len(outs)
    grouped = product.reshape(-1, xs, 8, product.shape[1])
    size = grouped.shape[0] * 8
    for there in range(xs):
        piece = grouped[:, there].reshape(size, -1)
        for d in range(xs):
            @pl.when(lax.rem(aux + d, xs) == there)
            def _():
                outs[d][row : row + size, col : col + piece.shape[1]] = piece


def wide(refs, core=None):
    parts = []
    for ref in refs:
        for q in range(ref.shape[0]):
            part = ref[q] if core is None else ref[q, :, core]
            parts.append(part.reshape(-1, part.shape[-1]))
    return jnp.concatenate(parts, axis=1)


def split_kernel(place, kept, got, *outs):
    store_by_aux(place[2], kept[...] + got[...], outs, 0, 0)


def early_kernel(place, mine, mine2, above, above2, below, below2, *outs):
    core, aux = place[0], place[2]
    n = above.shape[1] * above.shape[2] * above.shape[3]
    own, up = wide((mine, mine2), core), wide((above, above2), core)
    store_by_aux(aux, times_transposed(own, wide((above, above2))), outs, 0, 0)
    both = times_transposed(jnp.concatenate([up, own], axis=0), wide((below, below2)))
    store_by_aux(aux, both[: up.shape[0]], outs, 0, n)
    store_by_aux(aux, both[up.shape[0] :], outs, 0, 2 * n)


def late_kernel(place, below, below2, mine, mine2, above, above2, across, across2, _, *outs):
    core, aux = place[0], place[2]
    right = wide((across, across2))
    for at, slabs in enumerate(((below, below2), (mine, mine2), (above, above2))):
        product = times_transposed(wide(slabs, core), right)
        store_by_aux(aux, product, outs, at * (product.shape[0] // len(outs)), 0)


def pairs(kernel, place, operands, shape, xs, after=(), flops=1, limit=24 * MIB):
    out = jax.ShapeDtypeStruct(shape, jnp.float32)
    return pl.pallas_call(
        kernel,
        in_specs=[SCALARS] + [ANYWHERE] * len(operands) + [AFTER] * len(after),
        out_specs=[ANYWHERE] * xs,
        out_shape=[out] * xs,
        compiler_params=pltpu.CompilerParams(vmem_limit_bytes=limit),
        cost_estimate=pl.CostEstimate(flops=flops, bytes_accessed=1, transcendentals=0),
        name=kernel.__name__,
    )(place, *operands, *after)


def spread_kernel(ys, place, rows, out):
    peers = out.shape[0] // ys
    n = rows.shape[1] // 7
    size = n // peers
    out[...] = jnp.zeros_like(out)
    for step in range(1, ys):
        first = lax.rem(place[1] + step, ys) * peers
        for k in range(peers):
            begin = (ys - 1 + step) * n + k * size
            out[first + k, :, :size] = rows[:, begin : begin + size]


def finish_kernel(ys, place, rows, pieces, out):
    peers = pieces.shape[0] // ys
    n = out.shape[1] // ys
    zs = n // peers // 8
    for step in range(ys):
        owner = lax.rem(place[1] + step, ys)
        block = rows[:, step * n : (step + 1) * n]
        if step:
            came = [pieces[owner * peers + k] for k in range(peers)]
            parts = [came[k][:, at * 8 : (at + 1) * 8] for at in range(zs) for k in range(peers)]
            block = block + jnp.concatenate(parts, axis=1)
        out[:, pl.ds(pl.multiple_of(owner * n, n), n)] = block


def small(kernel, shape, *operands):
    ys = 4
    return pl.pallas_call(
        functools.partial(kernel, ys),
        in_specs=[SCALARS] + [ANYWHERE] * (len(operands) - 1),
        out_specs=ANYWHERE,
        out_shape=jax.ShapeDtypeStruct(shape, jnp.float32),
        compiler_params=pltpu.CompilerParams(vmem_limit_bytes=4 * MIB),
        cost_estimate=pl.CostEstimate(flops=1, bytes_accessed=1, transcendentals=0),
        name=kernel.__name__,
    )(*operands)


def over_aux(parts, xs):
    there = {d: shift(parts[d], "aux", d, xs) for d in (2, 1, 3)}
    return [parts[0], there[1], there[2], there[3]]


SLOTS = ((0,), (3,), (5,), (1, 6), (7, 4, 2))


def turn(block, zs):
    rows, cols = block.shape
    turned = block.T.reshape(zs, cols // zs // 8, 8, rows)
    return [[turned[at, k] for k in range(turned.shape[1])] for at in range(zs)]


def send_out(place, buffer, outs):
    zs = buffer.shape[0]
    for out, steps in zip(outs, SLOTS):
        for at, step in enumerate(steps):
            out[at] = buffer[lax.rem(place[3] + step, zs)]


def pack_kernel(place, *refs):
    diags, (early, third, middle, up, down), outs, buffer = refs[:4], refs[4:9], refs[9:-1], refs[-1]
    zs = buffer.shape[0]
    n = third.shape[1]
    buffer[:, :, :n] = (diags[0][...] + diags[1][...] + diags[2][...] + diags[3][...]).reshape(zs, 8, n)
    blocks = (early[:, :n] + up[...], third[...] + middle[...], early[:, 2 * n :] + down[...])
    for at, block in enumerate(blocks):
        buffer[:, :, (1 + at) * n : (2 + at) * n] = block.reshape(zs, 8, n)
        size = block.shape[0]
        for owner, pieces in enumerate(turn(block, zs)):
            for k, piece in enumerate(pieces):
                lane = (4 + at) * n + k * size
                buffer[owner, :, lane : lane + size] = piece
    send_out(place, buffer, outs)


def pack(place, *operands):
    zs = 8
    width = 7 * operands[0].shape[1]
    shapes = [(len(steps), 8, width) for steps in SLOTS]
    return pl.pallas_call(
        pack_kernel,
        in_specs=[SCALARS] + [ANYWHERE] * len(operands),
        out_specs=[ANYWHERE] * len(shapes),
        out_shape=[jax.ShapeDtypeStruct(s, jnp.float32) for s in shapes],
        scratch_shapes=[pltpu.VMEM((zs, 8, width), jnp.float32)],
        compiler_params=pltpu.CompilerParams(vmem_limit_bytes=8 * MIB),
        cost_estimate=pl.CostEstimate(flops=1, bytes_accessed=1, transcendentals=0),
        name="pack",
    )(place, *operands)


def first_z(packed):
    zs = 8
    here, forward, backward, up, down = packed
    up, down = shift(up, "z", 1, zs), shift(down, "z", -1, zs)
    return here[0] + up[0] + down[0], forward[0] + down[2], backward[0] + up[1] + down[1]


def second_z(here, forward, backward):
    zs = 8
    return here, shift(forward, "z", 3, zs), shift(backward, "z", -3, zs)


def total_kernel(waits, *refs):
    parts, out = refs[: len(refs) - 1 - waits], refs[-1]
    value = parts[0][...]
    for part in parts[1:]:
        value = value + part[...]
    out[...] = value


def total(parts, after=(), flops=1):
    return pl.pallas_call(
        functools.partial(total_kernel, len(after)),
        in_specs=[ANYWHERE] * len(parts) + [AFTER] * len(after),
        out_specs=ANYWHERE,
        out_shape=jax.ShapeDtypeStruct(parts[0].shape, parts[0].dtype),
        compiler_params=pltpu.CompilerParams(vmem_limit_bytes=4 * MIB),
        cost_estimate=pl.CostEstimate(flops=flops, bytes_accessed=1, transcendentals=0),
        name="total",
    )(*parts, *after)


def body(half_transformed, screen):
    qrows, mrows, icols = half_transformed.shape
    ys, zs, xs = 4, 8, 4
    quarter = qrows // ys
    row, z = lax.axis_index("row"), lax.axis_index("z")
    core, aux = lax.axis_index("core"), lax.axis_index("aux")
    place = jnp.stack([core, row, aux, z]).astype(jnp.int32)
    n = mrows
    tiles = mrows // TILE
    local = lax.dynamic_slice(screen, (aux * qrows, row * tiles), (qrows, tiles))
    keep = jnp.repeat(local, TILE, axis=1).astype(jnp.bfloat16)

    def slab(block, step):
        first = lax.rem(row + step, ys) * quarter
        part = lax.dynamic_slice(block, (first, 0, 0), (quarter, mrows, icols))
        return part * lax.dynamic_slice(keep, (first, 0), (quarter, mrows))[:, :, None]

    to_up, to_down = slab(half_transformed, 1), slab(half_transformed, 3)
    block, to_up, to_down = lax.optimization_barrier((half_transformed, to_up, to_down))
    below = shift(to_up, "row", 1, ys)
    above = shift(to_down, "row", -1, ys)
    mine, far = slab(block, 0), slab(block, 2)
    mine2 = sibling(mine)
    kept, given = diagonal(place, screen, block, zs)
    diag = pairs(split_kernel, place, (kept, sibling(given)), (zs * 8, n), xs, limit=4 * MIB)
    diag = over_aux(diag, xs)
    below, above, far, diag = lax.optimization_barrier((below, above, far, diag))
    across = shift(far, "row", 2, ys)

    def grouped(*slabs):
        return [s.reshape(quarter, zs, 2, n // zs // 2, icols) for s in slabs]

    mine, mine2 = grouped(mine, mine2)
    below, above = grouped(below, sibling(below)), grouped(above, sibling(above))
    early_parts = pairs(early_kernel, place, (mine, mine2, *above, *below), (zs * 8, 3 * n), xs)
    early = total(over_aux(early_parts, xs), flops=SOME)
    third = shift(early[:, n : 2 * n], "row", 1, ys)
    late_parts = pairs(
        late_kernel,
        place,
        (*below, mine, mine2, *above, *grouped(across, sibling(across))),
        (3 * zs * 8, n),
        xs,
        (early,),
    )
    late = total(over_aux(late_parts, xs), (third,))
    down, middle, up = late.reshape(3, zs * 8, n)
    up, down = shift(up, "row", 1, ys), shift(down, "row", -1, ys)
    rows = first_z(pack(place, *diag, early, third, middle, up, down))
    here, forward, backward = second_z(*rows)
    rows = here + forward + backward
    peers = 2 * xs
    pieces = small(spread_kernel, (ys * peers, 8, 128), place, rows)
    pieces = lax.all_to_all(pieces, ("row", "core", "aux"), 0, 0, tiled=True)
    return small(finish_kernel, (8, ys * n), place, rows, pieces)


def solution(mesh):
    rows, cols, aux = mesh.devices.shape
    split = Mesh(mesh.devices.reshape(rows, cols // 2, 2, aux), ("row", "z", "core", "aux"))
    in_specs = (P("aux", "row", ("z", "core")), P())
    out_specs = P(("row", "z", "core", "aux"), None)
    return jax.shard_map(body, mesh=split, in_specs=in_specs, out_specs=out_specs, check_vma=False)
```

```python
import functools

import jax
import jax.numpy as jnp
from jax import lax
from jax.experimental import pallas as pl
from jax.experimental.pallas import tpu as pltpu
from jax.sharding import Mesh, PartitionSpec as P

TILE = 128
MIB = 1024 * 1024
ANYWHERE = pl.BlockSpec(memory_space=pltpu.VMEM)
SOME = 10_000_000_000
LESS = 1_000_000_000
MORE = 6_000_000_000
AFTER = pl.BlockSpec(memory_space=pl.ANY)
SCALARS = pl.BlockSpec(memory_space=pltpu.SMEM)


def shift(value, axis, step, size):
    return lax.ppermute(value, axis, [(i, (i + step) % size) for i in range(size)])


def sibling(value):
    return lax.ppermute(value, "core", [(0, 1), (1, 0)])


def times_transposed(left, right):
    return lax.dot_general(left, right, (((1,), (1,)), ((), ())), preferred_element_type=jnp.float32)


def diagonal_kernel(place, screen, slab, keep, give, total):
    step = pl.program_id(0)
    core, row, aux = place[0], place[1], place[2]
    group, mrows, _ = slab.shape
    depth = pl.num_programs(0) * group
    tiles = mrows // TILE

    def masked(q):
        at = aux * depth + step * group + q
        parts = [
            slab[q, t * TILE : (t + 1) * TILE, :] * screen[at, row * tiles + t].astype(jnp.bfloat16)
            for t in range(tiles)
        ]
        return jnp.concatenate(parts, axis=0)

    rows = jnp.concatenate([masked(q) for q in range(group)], axis=1)
    product = times_transposed(rows, rows)

    @pl.when(step == 0)
    def _():
        total[...] = product.reshape(total.shape)

    @pl.when(step > 0)
    def _():
        total[...] += product.reshape(total.shape)

    @pl.when(step == pl.num_programs(0) - 1)
    def _():
        keep[...] = total[:, core].reshape(keep.shape)
        give[...] = total[:, 1 - core].reshape(give.shape)


def diagonal(place, screen, block, zs, group=4):
    depth, rows, width = block.shape
    half = jax.ShapeDtypeStruct((rows // 2, rows), jnp.float32)
    whole = pl.BlockSpec((rows // 2, rows), lambda q: (0, 0))
    return pl.pallas_call(
        diagonal_kernel,
        grid=(depth // group,),
        in_specs=[SCALARS, SCALARS, pl.BlockSpec((group, rows, width), lambda q: (q, 0, 0))],
        out_specs=[whole, whole],
        scratch_shapes=[pltpu.VMEM((zs, 2, rows // zs // 2, rows), jnp.float32)],
        out_shape=[half, half],
        compiler_params=pltpu.CompilerParams(vmem_limit_bytes=16 * MIB),
        cost_estimate=pl.CostEstimate(flops=1, bytes_accessed=1, transcendentals=0),
        name="diagonal",
    )(place, screen, block)


def store_by_aux(aux, product, outs, row, col):
    xs = len(outs)
    grouped = product.reshape(-1, xs, 8, product.shape[1])
    size = grouped.shape[0] * 8
    for there in range(xs):
        piece = grouped[:, there].reshape(size, -1)
        for d in range(xs):
            @pl.when(lax.rem(aux + d, xs) == there)
            def _():
                outs[d][row : row + size, col : col + piece.shape[1]] = piece


def wide(refs, core=None):
    parts = []
    for ref in refs:
        for q in range(ref.shape[0]):
            part = ref[q] if core is None else ref[q, :, core]
            parts.append(part.reshape(-1, part.shape[-1]))
    return jnp.concatenate(parts, axis=1)


def split_kernel(place, kept, got, *outs):
    store_by_aux(place[2], kept[...] + got[...], outs, 0, 0)


def early_kernel(place, mine, mine2, above, above2, below, below2, *outs):
    core, aux = place[0], place[2]
    n = above.shape[1] * above.shape[2] * above.shape[3]
    own, up = wide((mine, mine2), core), wide((above, above2), core)
    store_by_aux(aux, times_transposed(own, wide((above, above2))), outs, 0, 0)
    both = times_transposed(jnp.concatenate([up, own], axis=0), wide((below, below2)))
    store_by_aux(aux, both[: up.shape[0]], outs, 0, n)
    store_by_aux(aux, both[up.shape[0] :], outs, 0, 2 * n)


def late_kernel(place, below, mine, above, across, *refs):
    given, *outs = refs
    core, aux = place[0], place[2]
    left = [wide((slab,), core) for slab in (below, mine, above)]
    product = times_transposed(jnp.concatenate(left, axis=0), wide((across,)))
    size = left[0].shape[0]
    for at in range(3):
        rows = slice(at * size, (at + 1) * size)
        store_by_aux(aux, product[rows] + given[rows, :], outs, at * (size // len(outs)), 0)


def own_kernel(place, below, mine, above, across, _, out):
    core = place[0]
    left = [wide((slab,), core) for slab in (below, mine, above)]
    out[...] = times_transposed(jnp.concatenate(left, axis=0), wide((across,)))


def pairs(kernel, place, operands, shape, xs, after=(), flops=1, limit=24 * MIB):
    out = jax.ShapeDtypeStruct(shape, jnp.float32)
    return pl.pallas_call(
        kernel,
        in_specs=[SCALARS] + [ANYWHERE] * len(operands) + [AFTER] * len(after),
        out_specs=[ANYWHERE] * xs,
        out_shape=[out] * xs,
        compiler_params=pltpu.CompilerParams(vmem_limit_bytes=limit),
        cost_estimate=pl.CostEstimate(flops=flops, bytes_accessed=1, transcendentals=0),
        name=kernel.__name__,
    )(place, *operands, *after)


def spread_kernel(ys, place, rows, out):
    peers = out.shape[0] // ys
    n = rows.shape[1] // 7
    size = n // peers
    out[...] = jnp.zeros_like(out)
    for step in range(1, ys):
        first = lax.rem(place[1] + step, ys) * peers
        for k in range(peers):
            begin = (ys - 1 + step) * n + k * size
            out[first + k, :, :size] = rows[:, begin : begin + size]


def finish_kernel(ys, place, rows, pieces, out):
    peers = pieces.shape[0] // ys
    n = out.shape[1] // ys
    zs = n // peers // 8
    for step in range(ys):
        owner = lax.rem(place[1] + step, ys)
        block = rows[:, step * n : (step + 1) * n]
        if step:
            came = [pieces[owner * peers + k] for k in range(peers)]
            parts = [came[k][:, at * 8 : (at + 1) * 8] for at in range(zs) for k in range(peers)]
            block = block + jnp.concatenate(parts, axis=1)
        out[:, pl.ds(pl.multiple_of(owner * n, n), n)] = block


def small(kernel, shape, *operands):
    ys = 4
    return pl.pallas_call(
        functools.partial(kernel, ys),
        in_specs=[SCALARS] + [ANYWHERE] * (len(operands) - 1),
        out_specs=ANYWHERE,
        out_shape=jax.ShapeDtypeStruct(shape, jnp.float32),
        compiler_params=pltpu.CompilerParams(vmem_limit_bytes=4 * MIB),
        cost_estimate=pl.CostEstimate(flops=1, bytes_accessed=1, transcendentals=0),
        name=kernel.__name__,
    )(*operands)


def over_aux(parts, xs):
    there = {d: shift(parts[d], "aux", d, xs) for d in (2, 1, 3)}
    return [parts[0], there[2], there[3], there[1]]


def turn(block, zs):
    rows, cols = block.shape
    turned = block.T.reshape(zs, cols // zs // 8, 8, rows)
    return [[turned[at, k] for k in range(turned.shape[1])] for at in range(zs)]


def send_out(place, buffer, outs):
    zs, _, width = buffer.shape
    here, forward, backward, up, down = outs
    for out, step in ((here, 0), (forward, 3), (backward, 5)):
        out[...] = buffer[lax.rem(place[3] + step, zs)]
    for out, steps in ((up, (1, 6)), (down, (7, 2))):
        for at, step in enumerate(steps):
            out[:, at * width : (at + 1) * width] = buffer[lax.rem(place[3] + step, zs)]
    half = width // 2
    opposite = lax.rem(place[3] + zs // 2, zs)
    up[:, 2 * width :] = buffer[opposite, :, :half]
    down[:, 2 * width :] = buffer[opposite, :, half:]


def pack_kernel(place, *refs):
    diags, (early, third, middle, up, down), outs, buffer = refs[:4], refs[4:9], refs[9:-1], refs[-1]
    zs = buffer.shape[0]
    n = third.shape[1]
    buffer[:, :, :n] = (diags[0][...] + diags[1][...] + diags[2][...] + diags[3][...]).reshape(zs, 8, n)
    blocks = (early[:, :n] + up[...], third[...] + middle[...], early[:, 2 * n :] + down[...])
    for at, block in enumerate(blocks):
        buffer[:, :, (1 + at) * n : (2 + at) * n] = block.reshape(zs, 8, n)
        size = block.shape[0]
        for owner, pieces in enumerate(turn(block, zs)):
            for k, piece in enumerate(pieces):
                lane = (4 + at) * n + k * size
                buffer[owner, :, lane : lane + size] = piece
    send_out(place, buffer, outs)


def pack(place, *operands):
    zs = 8
    width = 7 * operands[0].shape[1]
    shapes = [(8, width)] * 3 + [(8, 2 * width + width // 2)] * 2
    return pl.pallas_call(
        pack_kernel,
        in_specs=[SCALARS] + [ANYWHERE] * len(operands),
        out_specs=[ANYWHERE] * len(shapes),
        out_shape=[jax.ShapeDtypeStruct(s, jnp.float32) for s in shapes],
        scratch_shapes=[pltpu.VMEM((zs, 8, width), jnp.float32)],
        compiler_params=pltpu.CompilerParams(vmem_limit_bytes=8 * MIB),
        cost_estimate=pl.CostEstimate(flops=1, bytes_accessed=1, transcendentals=0),
        name="pack",
    )(place, *operands)


def first_z(packed):
    zs = 8
    here, forward, backward, up, down = packed
    width = here.shape[1]
    half = width // 2
    up, down = shift(up, "z", 1, zs), shift(down, "z", -1, zs)
    here = here + up[:, :width] + down[:, :width]
    forward = forward + down[:, width : 2 * width]
    forward = jnp.concatenate([forward[:, :half] + up[:, 2 * width :], forward[:, half:]], axis=1)
    backward = backward + up[:, width : 2 * width]
    backward = jnp.concatenate([backward[:, :half], backward[:, half:] + down[:, 2 * width :]], axis=1)
    return here, forward, backward


def second_z(here, forward, backward):
    zs = 8
    return here, shift(forward, "z", 3, zs), shift(backward, "z", -3, zs)


def total_kernel(waits, *refs):
    parts, out = refs[: len(refs) - 1 - waits], refs[-1]
    value = parts[0][...]
    for part in parts[1:]:
        value = value + part[...]
    out[...] = value


def total(parts, after=(), flops=1):
    return pl.pallas_call(
        functools.partial(total_kernel, len(after)),
        in_specs=[ANYWHERE] * len(parts) + [AFTER] * len(after),
        out_specs=ANYWHERE,
        out_shape=jax.ShapeDtypeStruct(parts[0].shape, parts[0].dtype),
        compiler_params=pltpu.CompilerParams(vmem_limit_bytes=4 * MIB),
        cost_estimate=pl.CostEstimate(flops=flops, bytes_accessed=1, transcendentals=0),
        name="total",
    )(*parts, *after)


def body(half_transformed, screen):
    qrows, mrows, icols = half_transformed.shape
    ys, zs, xs = 4, 8, 4
    quarter = qrows // ys
    row, z = lax.axis_index("row"), lax.axis_index("z")
    core, aux = lax.axis_index("core"), lax.axis_index("aux")
    place = jnp.stack([core, row, aux, z]).astype(jnp.int32)
    n = mrows
    tiles = mrows // TILE
    local = lax.dynamic_slice(screen, (aux * qrows, row * tiles), (qrows, tiles))
    keep = jnp.repeat(local, TILE, axis=1).astype(jnp.bfloat16)

    def slab(block, step):
        first = lax.rem(row + step, ys) * quarter
        part = lax.dynamic_slice(block, (first, 0, 0), (quarter, mrows, icols))
        return part * lax.dynamic_slice(keep, (first, 0), (quarter, mrows))[:, :, None]

    to_up, to_down = slab(half_transformed, 1), slab(half_transformed, 3)
    block, to_up, to_down = lax.optimization_barrier((half_transformed, to_up, to_down))
    below = shift(to_up, "row", 1, ys)
    above = shift(to_down, "row", -1, ys)
    mine, far = slab(block, 0), slab(block, 2)
    mine2 = sibling(mine)
    kept, given = diagonal(place, screen, block, zs)
    diag = pairs(split_kernel, place, (kept, sibling(given)), (zs * 8, n), xs, limit=4 * MIB)
    diag = over_aux(diag, xs)
    below, above, far, diag = lax.optimization_barrier((below, above, far, diag))
    across = shift(far, "row", 2, ys)

    def grouped(*slabs):
        return [s.reshape(quarter, zs, 2, n // zs // 2, icols) for s in slabs]

    mine, mine2 = grouped(mine, mine2)
    below, above = grouped(below, sibling(below)), grouped(above, sibling(above))
    early_parts = pairs(early_kernel, place, (mine, mine2, *above, *below), (zs * 8, 3 * n), xs)
    early = total(over_aux(early_parts, xs), flops=SOME)
    third = shift(early[:, n : 2 * n], "row", 1, ys)
    (across_own,) = grouped(across)
    (across_sibling,) = grouped(sibling(across))
    (own,) = pairs(own_kernel, place, (below[0], mine, above[0], across_own), (3 * n // 2, n), 1, (early,))
    late_parts = pairs(
        late_kernel, place, (below[1], mine2, above[1], across_sibling, own), (3 * zs * 8, n), xs
    )
    late = total(over_aux(late_parts, xs), (third,))
    down, middle, up = late.reshape(3, zs * 8, n)
    up, down = shift(up, "row", 1, ys), shift(down, "row", -1, ys)
    rows = first_z(pack(place, *diag, early, third, middle, up, down))
    here, forward, backward = second_z(*rows)
    rows = here + forward + backward
    peers = 2 * xs
    pieces = small(spread_kernel, (ys * peers, 8, 128), place, rows)
    pieces = lax.all_to_all(pieces, ("row", "core", "aux"), 0, 0, tiled=True)
    return small(finish_kernel, (8, ys * n), place, rows, pieces)


def solution(mesh):
    rows, cols, aux = mesh.devices.shape
    split = Mesh(mesh.devices.reshape(rows, cols // 2, 2, aux), ("row", "z", "core", "aux"))
    in_specs = (P("aux", "row", ("z", "core")), P())
    out_specs = P(("row", "z", "core", "aux"), None)
    return jax.shard_map(body, mesh=split, in_specs=in_specs, out_specs=out_specs, check_vma=False)
```

```python
import functools

import jax
import jax.numpy as jnp
from jax import lax
from jax.experimental import pallas as pl
from jax.experimental.pallas import tpu as pltpu
from jax.sharding import Mesh, PartitionSpec as P

TILE = 128
MIB = 1024 * 1024
ANYWHERE = pl.BlockSpec(memory_space=pltpu.VMEM)
SOME = 10_000_000_000
LESS = 1_000_000_000
MORE = 6_000_000_000
AFTER = pl.BlockSpec(memory_space=pl.ANY)
SCALARS = pl.BlockSpec(memory_space=pltpu.SMEM)


def shift(value, axis, step, size):
    return lax.ppermute(value, axis, [(i, (i + step) % size) for i in range(size)])


def sibling(value):
    return lax.ppermute(value, "core", [(0, 1), (1, 0)])


def times_transposed(left, right):
    return lax.dot_general(left, right, (((1,), (1,)), ((), ())), preferred_element_type=jnp.float32)


def diagonal_kernel(place, screen, slab, keep, give, total):
    step = pl.program_id(0)
    core, row, aux = place[0], place[1], place[2]
    group, mrows, _ = slab.shape
    depth = pl.num_programs(0) * group
    tiles = mrows // TILE

    def masked(q):
        at = aux * depth + step * group + q
        parts = [
            slab[q, t * TILE : (t + 1) * TILE, :] * screen[at, row * tiles + t].astype(jnp.bfloat16)
            for t in range(tiles)
        ]
        return jnp.concatenate(parts, axis=0)

    rows = jnp.concatenate([masked(q) for q in range(group)], axis=1)
    product = times_transposed(rows, rows)

    @pl.when(step == 0)
    def _():
        total[...] = product.reshape(total.shape)

    @pl.when(step > 0)
    def _():
        total[...] += product.reshape(total.shape)

    @pl.when(step == pl.num_programs(0) - 1)
    def _():
        keep[...] = total[:, core].reshape(keep.shape)
        give[...] = total[:, 1 - core].reshape(give.shape)


def diagonal(place, screen, block, zs, group=4):
    depth, rows, width = block.shape
    half = jax.ShapeDtypeStruct((rows // 2, rows), jnp.float32)
    whole = pl.BlockSpec((rows // 2, rows), lambda q: (0, 0))
    return pl.pallas_call(
        diagonal_kernel,
        grid=(depth // group,),
        in_specs=[SCALARS, SCALARS, pl.BlockSpec((group, rows, width), lambda q: (q, 0, 0))],
        out_specs=[whole, whole],
        scratch_shapes=[pltpu.VMEM((zs, 2, rows // zs // 2, rows), jnp.float32)],
        out_shape=[half, half],
        compiler_params=pltpu.CompilerParams(vmem_limit_bytes=16 * MIB),
        cost_estimate=pl.CostEstimate(flops=1, bytes_accessed=1, transcendentals=0),
        name="diagonal",
    )(place, screen, block)


def store_by_aux(aux, product, outs, row, col):
    xs = len(outs)
    grouped = product.reshape(-1, xs, 8, product.shape[1])
    size = grouped.shape[0] * 8
    for there in range(xs):
        piece = grouped[:, there].reshape(size, -1)
        for d in range(xs):
            @pl.when(lax.rem(aux + d, xs) == there)
            def _():
                outs[d][row : row + size, col : col + piece.shape[1]] = piece


def wide(refs, core=None):
    parts = []
    for ref in refs:
        for q in range(ref.shape[0]):
            part = ref[q] if core is None else ref[q, :, core]
            parts.append(part.reshape(-1, part.shape[-1]))
    return jnp.concatenate(parts, axis=1)


def split_kernel(place, kept, got, *outs):
    store_by_aux(place[2], kept[...] + got[...], outs, 0, 0)


def early_kernel(place, mine, mine2, above, above2, below, below2, *outs):
    core, aux = place[0], place[2]
    n = above.shape[1] * above.shape[2] * above.shape[3]
    own, up = wide((mine, mine2), core), wide((above, above2), core)
    store_by_aux(aux, times_transposed(own, wide((above, above2))), outs, 0, 0)
    both = times_transposed(jnp.concatenate([up, own], axis=0), wide((below, below2)))
    store_by_aux(aux, both[: up.shape[0]], outs, 0, n)
    store_by_aux(aux, both[up.shape[0] :], outs, 0, 2 * n)


def late_kernel(place, below, mine, above, across, *refs):
    given, *outs = refs
    core, aux = place[0], place[2]
    left = [wide((slab,), core) for slab in (below, mine, above)]
    product = times_transposed(jnp.concatenate(left, axis=0), wide((across,)))
    size = left[0].shape[0]
    outer, middle = outs[: len(outs) // 2], outs[len(outs) // 2 :]
    for at, (to, row) in enumerate(((outer, 0), (middle, 0), (outer, middle[0].shape[0]))):
        rows = slice(at * size, (at + 1) * size)
        store_by_aux(aux, product[rows] + given[rows, :], to, row, 0)


def own_kernel(place, below, mine, above, across, _, out):
    core = place[0]
    left = [wide((slab,), core) for slab in (below, mine, above)]
    out[...] = times_transposed(jnp.concatenate(left, axis=0), wide((across,)))


def pairs(kernel, place, operands, shapes, after=(), flops=1, limit=24 * MIB):
    return pl.pallas_call(
        kernel,
        in_specs=[SCALARS] + [ANYWHERE] * len(operands) + [AFTER] * len(after),
        out_specs=[ANYWHERE] * len(shapes),
        out_shape=[jax.ShapeDtypeStruct(shape, jnp.float32) for shape in shapes],
        compiler_params=pltpu.CompilerParams(vmem_limit_bytes=limit),
        cost_estimate=pl.CostEstimate(flops=flops, bytes_accessed=1, transcendentals=0),
        name=kernel.__name__,
    )(place, *operands, *after)


def spread_kernel(ys, place, rows, out):
    peers = out.shape[0] // ys
    n = rows.shape[1] // 7
    size = n // peers
    out[...] = jnp.zeros_like(out)
    for step in range(1, ys):
        first = lax.rem(place[1] + step, ys) * peers
        for k in range(peers):
            begin = (ys - 1 + step) * n + k * size
            out[first + k, :, :size] = rows[:, begin : begin + size]


def finish_kernel(ys, place, rows, pieces, out):
    peers = pieces.shape[0] // ys
    n = out.shape[1] // ys
    zs = n // peers // 8
    for step in range(ys):
        owner = lax.rem(place[1] + step, ys)
        block = rows[:, step * n : (step + 1) * n]
        if step:
            came = [pieces[owner * peers + k] for k in range(peers)]
            parts = [came[k][:, at * 8 : (at + 1) * 8] for at in range(zs) for k in range(peers)]
            block = block + jnp.concatenate(parts, axis=1)
        out[:, pl.ds(pl.multiple_of(owner * n, n), n)] = block


def small(kernel, shape, *operands):
    ys = 4
    return pl.pallas_call(
        functools.partial(kernel, ys),
        in_specs=[SCALARS] + [ANYWHERE] * (len(operands) - 1),
        out_specs=ANYWHERE,
        out_shape=jax.ShapeDtypeStruct(shape, jnp.float32),
        compiler_params=pltpu.CompilerParams(vmem_limit_bytes=4 * MIB),
        cost_estimate=pl.CostEstimate(flops=1, bytes_accessed=1, transcendentals=0),
        name=kernel.__name__,
    )(*operands)


def over_aux(parts, xs):
    there = {d: shift(parts[d], "aux", d, xs) for d in (2, 1, 3)}
    return [parts[0], there[2], there[3], there[1]]


def turn(block, zs):
    rows, cols = block.shape
    turned = block.T.reshape(zs, cols // zs // 8, 8, rows)
    return [[turned[at, k] for k in range(turned.shape[1])] for at in range(zs)]


def send_out(place, buffer, outs):
    zs, _, width = buffer.shape
    here, forward, backward, up, down = outs
    for out, step in ((here, 0), (forward, 3), (backward, 5)):
        out[...] = buffer[lax.rem(place[3] + step, zs)]
    for out, steps in ((up, (1, 6)), (down, (7, 2))):
        for at, step in enumerate(steps):
            out[:, at * width : (at + 1) * width] = buffer[lax.rem(place[3] + step, zs)]
    half = width // 2
    opposite = lax.rem(place[3] + zs // 2, zs)
    up[:, 2 * width :] = buffer[opposite, :, :half]
    down[:, 2 * width :] = buffer[opposite, :, half:]


def pack_kernel(place, *refs):
    diags, (early, third, middle, up, down), outs, buffer = refs[:4], refs[4:9], refs[9:-1], refs[-1]
    zs = buffer.shape[0]
    n = third.shape[1]
    buffer[:, :, :n] = (diags[0][...] + diags[1][...] + diags[2][...] + diags[3][...]).reshape(zs, 8, n)
    blocks = (early[:, :n] + up[...], third[...] + middle[...], early[:, 2 * n :] + down[...])
    for at, block in enumerate(blocks):
        buffer[:, :, (1 + at) * n : (2 + at) * n] = block.reshape(zs, 8, n)
        size = block.shape[0]
        for owner, pieces in enumerate(turn(block, zs)):
            for k, piece in enumerate(pieces):
                lane = (4 + at) * n + k * size
                buffer[owner, :, lane : lane + size] = piece
    send_out(place, buffer, outs)


def pack(place, *operands):
    zs = 8
    width = 7 * operands[0].shape[1]
    shapes = [(8, width)] * 3 + [(8, 2 * width + width // 2)] * 2
    return pl.pallas_call(
        pack_kernel,
        in_specs=[SCALARS] + [ANYWHERE] * len(operands),
        out_specs=[ANYWHERE] * len(shapes),
        out_shape=[jax.ShapeDtypeStruct(s, jnp.float32) for s in shapes],
        scratch_shapes=[pltpu.VMEM((zs, 8, width), jnp.float32)],
        compiler_params=pltpu.CompilerParams(vmem_limit_bytes=8 * MIB),
        cost_estimate=pl.CostEstimate(flops=1, bytes_accessed=1, transcendentals=0),
        name="pack",
    )(place, *operands)


def first_z(packed):
    zs = 8
    here, forward, backward, up, down = packed
    width = here.shape[1]
    half = width // 2
    up, down = shift(up, "z", 1, zs), shift(down, "z", -1, zs)
    here = here + up[:, :width] + down[:, :width]
    forward = forward + down[:, width : 2 * width]
    forward = jnp.concatenate([forward[:, :half] + up[:, 2 * width :], forward[:, half:]], axis=1)
    backward = backward + up[:, width : 2 * width]
    backward = jnp.concatenate([backward[:, :half], backward[:, half:] + down[:, 2 * width :]], axis=1)
    return here, forward, backward


def second_z(here, forward, backward):
    zs = 8
    return here, shift(forward, "z", 3, zs), shift(backward, "z", -3, zs)


def total_kernel(waits, *refs):
    parts, out = refs[: len(refs) - 1 - waits], refs[-1]
    value = parts[0][...]
    for part in parts[1:]:
        value = value + part[...]
    out[...] = value


def total(parts, after=(), flops=1):
    return pl.pallas_call(
        functools.partial(total_kernel, len(after)),
        in_specs=[ANYWHERE] * len(parts) + [AFTER] * len(after),
        out_specs=ANYWHERE,
        out_shape=jax.ShapeDtypeStruct(parts[0].shape, parts[0].dtype),
        compiler_params=pltpu.CompilerParams(vmem_limit_bytes=4 * MIB),
        cost_estimate=pl.CostEstimate(flops=flops, bytes_accessed=1, transcendentals=0),
        name="total",
    )(*parts, *after)


def body(half_transformed, screen):
    qrows, mrows, icols = half_transformed.shape
    ys, zs, xs = 4, 8, 4
    quarter = qrows // ys
    row, z = lax.axis_index("row"), lax.axis_index("z")
    core, aux = lax.axis_index("core"), lax.axis_index("aux")
    place = jnp.stack([core, row, aux, z]).astype(jnp.int32)
    n = mrows
    tiles = mrows // TILE
    local = lax.dynamic_slice(screen, (aux * qrows, row * tiles), (qrows, tiles))
    keep = jnp.repeat(local, TILE, axis=1).astype(jnp.bfloat16)

    def slab(block, step):
        first = lax.rem(row + step, ys) * quarter
        part = lax.dynamic_slice(block, (first, 0, 0), (quarter, mrows, icols))
        return part * lax.dynamic_slice(keep, (first, 0), (quarter, mrows))[:, :, None]

    to_up, to_down = slab(half_transformed, 1), slab(half_transformed, 3)
    block, to_up, to_down = lax.optimization_barrier((half_transformed, to_up, to_down))
    below = shift(to_up, "row", 1, ys)
    above = shift(to_down, "row", -1, ys)
    mine, far = slab(block, 0), slab(block, 2)
    mine2 = sibling(mine)
    kept, given = diagonal(place, screen, block, zs)
    diag = pairs(split_kernel, place, (kept, sibling(given)), [(zs * 8, n)] * xs, limit=4 * MIB)
    diag = over_aux(diag, xs)
    below, above, far, diag = lax.optimization_barrier((below, above, far, diag))
    across = shift(far, "row", 2, ys)

    def grouped(*slabs):
        return [s.reshape(quarter, zs, 2, n // zs // 2, icols) for s in slabs]

    mine, mine2 = grouped(mine, mine2)
    below, above = grouped(below, sibling(below)), grouped(above, sibling(above))
    early_parts = pairs(early_kernel, place, (mine, mine2, *above, *below), [(zs * 8, 3 * n)] * xs)
    early = total(over_aux(early_parts, xs), flops=SOME)
    third = shift(early[:, n : 2 * n], "row", 1, ys)
    (across_own,) = grouped(across)
    (across_sibling,) = grouped(sibling(across))
    (own,) = pairs(own_kernel, place, (below[0], mine, above[0], across_own), [(3 * n // 2, n)], (early,))
    shapes = [(2 * zs * 8, n)] * xs + [(zs * 8, n)] * xs
    late_parts = pairs(late_kernel, place, (below[1], mine2, above[1], across_sibling, own), shapes)
    outer = total(over_aux(late_parts[:xs], xs), (third,))
    middle = total(over_aux(late_parts[xs:], xs))
    up, down = shift(outer[zs * 8 :], "row", 1, ys), shift(outer[: zs * 8], "row", -1, ys)
    rows = first_z(pack(place, *diag, early, third, middle, up, down))
    here, forward, backward = second_z(*rows)
    rows = here + forward + backward
    peers = 2 * xs
    pieces = small(spread_kernel, (ys * peers, 8, 128), place, rows)
    pieces = lax.all_to_all(pieces, ("row", "core", "aux"), 0, 0, tiled=True)
    return small(finish_kernel, (8, ys * n), place, rows, pieces)


def solution(mesh):
    rows, cols, aux = mesh.devices.shape
    split = Mesh(mesh.devices.reshape(rows, cols // 2, 2, aux), ("row", "z", "core", "aux"))
    in_specs = (P("aux", "row", ("z", "core")), P())
    out_specs = P(("row", "z", "core", "aux"), None)
    return jax.shard_map(body, mesh=split, in_specs=in_specs, out_specs=out_specs, check_vma=False)
```

```python
import functools

import jax
import jax.numpy as jnp
from jax import lax
from jax.experimental import pallas as pl
from jax.experimental.pallas import tpu as pltpu
from jax.sharding import Mesh, PartitionSpec as P

TILE = 128
MIB = 1024 * 1024
ANYWHERE = pl.BlockSpec(memory_space=pltpu.VMEM)
SOME = 10_000_000_000
LESS = 1_000_000_000
MORE = 6_000_000_000
AFTER = pl.BlockSpec(memory_space=pl.ANY)
SCALARS = pl.BlockSpec(memory_space=pltpu.SMEM)


def shift(value, axis, step, size):
    return lax.ppermute(value, axis, [(i, (i + step) % size) for i in range(size)])


def sibling(value):
    return lax.ppermute(value, "core", [(0, 1), (1, 0)])


def times_transposed(left, right):
    return lax.dot_general(left, right, (((1,), (1,)), ((), ())), preferred_element_type=jnp.float32)


def diagonal_kernel(place, screen, slab, keep, give, total):
    step = pl.program_id(0)
    core, row, aux = place[0], place[1], place[2]
    group, mrows, _ = slab.shape
    depth = pl.num_programs(0) * group
    tiles = mrows // TILE

    def masked(q):
        at = aux * depth + step * group + q
        parts = [
            slab[q, t * TILE : (t + 1) * TILE, :] * screen[at, row * tiles + t].astype(jnp.bfloat16)
            for t in range(tiles)
        ]
        return jnp.concatenate(parts, axis=0)

    rows = jnp.concatenate([masked(q) for q in range(group)], axis=1)
    product = times_transposed(rows, rows)

    @pl.when(step == 0)
    def _():
        total[...] = product.reshape(total.shape)

    @pl.when(step > 0)
    def _():
        total[...] += product.reshape(total.shape)

    @pl.when(step == pl.num_programs(0) - 1)
    def _():
        keep[...] = total[:, core].reshape(keep.shape)
        give[...] = total[:, 1 - core].reshape(give.shape)


def diagonal(place, screen, block, zs, group=4):
    depth, rows, width = block.shape
    half = jax.ShapeDtypeStruct((rows // 2, rows), jnp.float32)
    whole = pl.BlockSpec((rows // 2, rows), lambda q: (0, 0))
    return pl.pallas_call(
        diagonal_kernel,
        grid=(depth // group,),
        in_specs=[SCALARS, SCALARS, pl.BlockSpec((group, rows, width), lambda q: (q, 0, 0))],
        out_specs=[whole, whole],
        scratch_shapes=[pltpu.VMEM((zs, 2, rows // zs // 2, rows), jnp.float32)],
        out_shape=[half, half],
        compiler_params=pltpu.CompilerParams(vmem_limit_bytes=16 * MIB),
        cost_estimate=pl.CostEstimate(flops=1, bytes_accessed=1, transcendentals=0),
        name="diagonal",
    )(place, screen, block)


def store_by_aux(aux, product, outs, row, col):
    xs = len(outs)
    grouped = product.reshape(-1, xs, 8, product.shape[1])
    size = grouped.shape[0] * 8
    for there in range(xs):
        piece = grouped[:, there].reshape(size, -1)
        for d in range(xs):
            @pl.when(lax.rem(aux + d, xs) == there)
            def _():
                outs[d][row : row + size, col : col + piece.shape[1]] = piece


def wide(refs, core=None):
    parts = []
    for ref in refs:
        for q in range(ref.shape[0]):
            part = ref[q] if core is None else ref[q, :, core]
            parts.append(part.reshape(-1, part.shape[-1]))
    return jnp.concatenate(parts, axis=1)


def split_kernel(place, kept, got, *outs):
    store_by_aux(place[2], kept[...] + got[...], outs, 0, 0)


def early_kernel(place, mine, mine2, above, above2, below, below2, *outs):
    core, aux = place[0], place[2]
    n = above.shape[1] * above.shape[2] * above.shape[3]
    own, up = wide((mine, mine2), core), wide((above, above2), core)
    store_by_aux(aux, times_transposed(own, wide((above, above2))), outs, 0, 0)
    both = times_transposed(jnp.concatenate([up, own], axis=0), wide((below, below2)))
    store_by_aux(aux, both[: up.shape[0]], outs, 0, n)
    store_by_aux(aux, both[up.shape[0] :], outs, 0, 2 * n)


def late_kernel(place, below, mine, above, across, *refs):
    given, *outs = refs
    core, aux = place[0], place[2]
    left = [wide((slab,), core) for slab in (below, mine, above)]
    product = times_transposed(jnp.concatenate(left, axis=0), wide((across,)))
    size = left[0].shape[0]
    outer, middle = outs[: len(outs) // 2], outs[len(outs) // 2 :]
    for at, (to, row) in enumerate(((outer, 0), (middle, 0), (outer, middle[0].shape[0]))):
        rows = slice(at * size, (at + 1) * size)
        store_by_aux(aux, product[rows] + given[rows, :], to, row, 0)


def own_kernel(place, below, mine, above, across, _, out):
    core = place[0]
    left = [wide((slab,), core) for slab in (below, mine, above)]
    out[...] = times_transposed(jnp.concatenate(left, axis=0), wide((across,)))


def pairs(kernel, place, operands, shapes, after=(), flops=1, limit=24 * MIB):
    return pl.pallas_call(
        kernel,
        in_specs=[SCALARS] + [ANYWHERE] * len(operands) + [AFTER] * len(after),
        out_specs=[ANYWHERE] * len(shapes),
        out_shape=[jax.ShapeDtypeStruct(shape, jnp.float32) for shape in shapes],
        compiler_params=pltpu.CompilerParams(vmem_limit_bytes=limit),
        cost_estimate=pl.CostEstimate(flops=flops, bytes_accessed=1, transcendentals=0),
        name=kernel.__name__,
    )(place, *operands, *after)


def spread_kernel(ys, place, rows, out):
    peers = out.shape[0] // ys
    n = rows.shape[1] // 7
    size = n // peers
    for step in range(1, ys):
        first = lax.rem(place[1] + step, ys) * peers
        for k in range(peers):
            begin = (ys - 1 + step) * n + k * size
            out[first + k, :, :size] = rows[:, begin : begin + size]
            out[first + k, :, size:] = jnp.zeros((8, out.shape[2] - size), jnp.float32)
    for k in range(peers):
        out[place[1] * peers + k] = jnp.zeros(out.shape[1:], jnp.float32)


def finish_kernel(ys, place, rows, pieces, out):
    peers = pieces.shape[0] // ys
    n = out.shape[1] // ys
    zs = n // peers // 8
    for step in range(ys):
        owner = lax.rem(place[1] + step, ys)
        block = rows[:, step * n : (step + 1) * n]
        if step:
            came = [pieces[owner * peers + k] for k in range(peers)]
            parts = [came[k][:, at * 8 : (at + 1) * 8] for at in range(zs) for k in range(peers)]
            block = block + jnp.concatenate(parts, axis=1)
        out[:, pl.ds(pl.multiple_of(owner * n, n), n)] = block


def small(kernel, shape, *operands):
    ys = 4
    return pl.pallas_call(
        functools.partial(kernel, ys),
        in_specs=[SCALARS] + [ANYWHERE] * (len(operands) - 1),
        out_specs=ANYWHERE,
        out_shape=jax.ShapeDtypeStruct(shape, jnp.float32),
        compiler_params=pltpu.CompilerParams(vmem_limit_bytes=4 * MIB),
        cost_estimate=pl.CostEstimate(flops=1, bytes_accessed=1, transcendentals=0),
        name=kernel.__name__,
    )(*operands)


def over_aux(parts, xs, order=(2, 3, 1)):
    there = {d: shift(parts[d], "aux", d, xs) for d in (2, 1, 3)}
    return [parts[0], *(there[d] for d in order)]


def turn(block, zs):
    rows, cols = block.shape
    turned = block.T.reshape(zs, cols // zs // 8, 8, rows)
    return [[turned[at, k] for k in range(turned.shape[1])] for at in range(zs)]


def send_out(place, buffer, outs):
    zs, _, width = buffer.shape
    here, forward, backward, up, down = outs
    for out, step in ((here, 0), (forward, 3), (backward, 5)):
        out[...] = buffer[lax.rem(place[3] + step, zs)]
    for out, steps in ((up, (1, 6)), (down, (7, 2))):
        for at, step in enumerate(steps):
            out[:, at * width : (at + 1) * width] = buffer[lax.rem(place[3] + step, zs)]
    half = width // 2
    opposite = lax.rem(place[3] + zs // 2, zs)
    up[:, 2 * width :] = buffer[opposite, :, :half]
    down[:, 2 * width :] = buffer[opposite, :, half:]


def pack_kernel(place, *refs):
    diags, (early, third, middle, up, down), outs, buffer = refs[:4], refs[4:9], refs[9:-1], refs[-1]
    zs = buffer.shape[0]
    n = third.shape[1]
    buffer[:, :, :n] = (diags[0][...] + diags[1][...] + diags[2][...] + diags[3][...]).reshape(zs, 8, n)
    blocks = (early[:, :n] + up[...], third[...] + middle[...], early[:, 2 * n :] + down[...])
    for at, block in enumerate(blocks):
        buffer[:, :, (1 + at) * n : (2 + at) * n] = block.reshape(zs, 8, n)
        size = block.shape[0]
        for owner, pieces in enumerate(turn(block, zs)):
            for k, piece in enumerate(pieces):
                lane = (4 + at) * n + k * size
                buffer[owner, :, lane : lane + size] = piece
    send_out(place, buffer, outs)


def pack(place, *operands):
    zs = 8
    width = 7 * operands[0].shape[1]
    shapes = [(8, width)] * 3 + [(8, 2 * width + width // 2)] * 2
    return pl.pallas_call(
        pack_kernel,
        in_specs=[SCALARS] + [ANYWHERE] * len(operands),
        out_specs=[ANYWHERE] * len(shapes),
        out_shape=[jax.ShapeDtypeStruct(s, jnp.float32) for s in shapes],
        scratch_shapes=[pltpu.VMEM((zs, 8, width), jnp.float32)],
        compiler_params=pltpu.CompilerParams(vmem_limit_bytes=8 * MIB),
        cost_estimate=pl.CostEstimate(flops=1, bytes_accessed=1, transcendentals=0),
        name="pack",
    )(place, *operands)


def first_z(packed):
    zs = 8
    here, forward, backward, up, down = packed
    width = here.shape[1]
    half = width // 2
    up, down = shift(up, "z", 1, zs), shift(down, "z", -1, zs)
    here = here + up[:, :width] + down[:, :width]
    forward = forward + down[:, width : 2 * width]
    forward = jnp.concatenate([forward[:, :half] + up[:, 2 * width :], forward[:, half:]], axis=1)
    backward = backward + up[:, width : 2 * width]
    backward = jnp.concatenate([backward[:, :half], backward[:, half:] + down[:, 2 * width :]], axis=1)
    return here, forward, backward


def second_z(here, forward, backward):
    zs = 8
    return here, shift(forward, "z", 3, zs), shift(backward, "z", -3, zs)


def total_kernel(waits, *refs):
    parts, out = refs[: len(refs) - 1 - waits], refs[-1]
    value = parts[0][...]
    for part in parts[1:]:
        value = value + part[...]
    out[...] = value


def total(parts, after=(), flops=1):
    return pl.pallas_call(
        functools.partial(total_kernel, len(after)),
        in_specs=[ANYWHERE] * len(parts) + [AFTER] * len(after),
        out_specs=ANYWHERE,
        out_shape=jax.ShapeDtypeStruct(parts[0].shape, parts[0].dtype),
        compiler_params=pltpu.CompilerParams(vmem_limit_bytes=4 * MIB),
        cost_estimate=pl.CostEstimate(flops=flops, bytes_accessed=1, transcendentals=0),
        name="total",
    )(*parts, *after)


def body(half_transformed, screen):
    qrows, mrows, icols = half_transformed.shape
    ys, zs, xs = 4, 8, 4
    quarter = qrows // ys
    row, z = lax.axis_index("row"), lax.axis_index("z")
    core, aux = lax.axis_index("core"), lax.axis_index("aux")
    place = jnp.stack([core, row, aux, z]).astype(jnp.int32)
    n = mrows
    tiles = mrows // TILE
    local = lax.dynamic_slice(screen, (aux * qrows, row * tiles), (qrows, tiles))
    keep = jnp.repeat(local, TILE, axis=1).astype(jnp.bfloat16)

    def slab(block, step):
        first = lax.rem(row + step, ys) * quarter
        part = lax.dynamic_slice(block, (first, 0, 0), (quarter, mrows, icols))
        return part * lax.dynamic_slice(keep, (first, 0), (quarter, mrows))[:, :, None]

    to_up, to_down = slab(half_transformed, 1), slab(half_transformed, 3)
    block, to_up, to_down = lax.optimization_barrier((half_transformed, to_up, to_down))
    below = shift(to_up, "row", 1, ys)
    above = shift(to_down, "row", -1, ys)
    mine, far = slab(block, 0), slab(block, 2)
    mine2 = sibling(mine)
    kept, given = diagonal(place, screen, block, zs)
    diag = pairs(split_kernel, place, (kept, sibling(given)), [(zs * 8, n)] * xs, limit=4 * MIB)
    diag = over_aux(diag, xs, (1, 2, 3))
    below, above, far, diag = lax.optimization_barrier((below, above, far, diag))
    across = shift(far, "row", 2, ys)

    def grouped(*slabs):
        return [s.reshape(quarter, zs, 2, n // zs // 2, icols) for s in slabs]

    mine, mine2 = grouped(mine, mine2)
    below, above = grouped(below, sibling(below)), grouped(above, sibling(above))
    early_parts = pairs(early_kernel, place, (mine, mine2, *above, *below), [(zs * 8, 3 * n)] * xs)
    early = total(over_aux(early_parts, xs, (1, 2, 3)), flops=SOME)
    third = shift(early[:, n : 2 * n], "row", 1, ys)
    (across_own,) = grouped(across)
    (across_sibling,) = grouped(sibling(across))
    (own,) = pairs(own_kernel, place, (below[0], mine, above[0], across_own), [(3 * n // 2, n)], (early,))
    shapes = [(2 * zs * 8, n)] * xs + [(zs * 8, n)] * xs
    late_parts = pairs(late_kernel, place, (below[1], mine2, above[1], across_sibling, own), shapes)
    outer = total(over_aux(late_parts[:xs], xs), (third,))
    middle = total(over_aux(late_parts[xs:], xs))
    up, down = shift(outer[zs * 8 :], "row", 1, ys), shift(outer[: zs * 8], "row", -1, ys)
    rows = first_z(pack(place, *diag, early, third, middle, up, down))
    here, forward, backward = second_z(*rows)
    rows = here + forward + backward
    peers = 2 * xs
    pieces = small(spread_kernel, (ys * peers, 8, 128), place, rows)
    pieces = lax.all_to_all(pieces, ("row", "core", "aux"), 0, 0, tiled=True)
    return small(finish_kernel, (8, ys * n), place, rows, pieces)


def solution(mesh):
    rows, cols, aux = mesh.devices.shape
    split = Mesh(mesh.devices.reshape(rows, cols // 2, 2, aux), ("row", "z", "core", "aux"))
    in_specs = (P("aux", "row", ("z", "core")), P())
    out_specs = P(("row", "z", "core", "aux"), None)
    return jax.shard_map(body, mesh=split, in_specs=in_specs, out_specs=out_specs, check_vma=False)
```

```python
import functools

import jax
import jax.numpy as jnp
from jax import lax
from jax.experimental import pallas as pl
from jax.experimental.pallas import tpu as pltpu
from jax.sharding import Mesh, PartitionSpec as P

TILE = 128
MIB = 1024 * 1024
ANYWHERE = pl.BlockSpec(memory_space=pltpu.VMEM)
SOME = 10_000_000_000
LESS = 1_000_000_000
MORE = 6_000_000_000
AFTER = pl.BlockSpec(memory_space=pl.ANY)
SCALARS = pl.BlockSpec(memory_space=pltpu.SMEM)


def shift(value, axis, step, size):
    return lax.ppermute(value, axis, [(i, (i + step) % size) for i in range(size)])


def sibling(value):
    return lax.ppermute(value, "core", [(0, 1), (1, 0)])


def times_transposed(left, right):
    return lax.dot_general(left, right, (((1,), (1,)), ((), ())), preferred_element_type=jnp.float32)


def diagonal_kernel(place, screen, slab, keep, give, total):
    step = pl.program_id(0)
    core, row, aux = place[0], place[1], place[2]
    group, mrows, _ = slab.shape
    depth = pl.num_programs(0) * group
    tiles = mrows // TILE

    def masked(q):
        at = aux * depth + step * group + q
        parts = [
            slab[q, t * TILE : (t + 1) * TILE, :] * screen[at, row * tiles + t].astype(jnp.bfloat16)
            for t in range(tiles)
        ]
        return jnp.concatenate(parts, axis=0)

    rows = jnp.concatenate([masked(q) for q in range(group)], axis=1)
    product = times_transposed(rows, rows)

    @pl.when(step == 0)
    def _():
        total[...] = product.reshape(total.shape)

    @pl.when(step > 0)
    def _():
        total[...] += product.reshape(total.shape)

    @pl.when(step == pl.num_programs(0) - 1)
    def _():
        keep[...] = total[:, core].reshape(keep.shape)
        give[...] = total[:, 1 - core].reshape(give.shape)


def diagonal(place, screen, block, zs, group=4):
    depth, rows, width = block.shape
    half = jax.ShapeDtypeStruct((rows // 2, rows), jnp.float32)
    whole = pl.BlockSpec((rows // 2, rows), lambda q: (0, 0))
    return pl.pallas_call(
        diagonal_kernel,
        grid=(depth // group,),
        in_specs=[SCALARS, SCALARS, pl.BlockSpec((group, rows, width), lambda q: (q, 0, 0))],
        out_specs=[whole, whole],
        scratch_shapes=[pltpu.VMEM((zs, 2, rows // zs // 2, rows), jnp.float32)],
        out_shape=[half, half],
        compiler_params=pltpu.CompilerParams(vmem_limit_bytes=16 * MIB),
        cost_estimate=pl.CostEstimate(flops=1, bytes_accessed=1, transcendentals=0),
        name="diagonal",
    )(place, screen, block)


def store_by_aux(aux, product, outs, row, col):
    xs = len(outs)
    grouped = product.reshape(-1, xs, 8, product.shape[1])
    size = grouped.shape[0] * 8
    for there in range(xs):
        piece = grouped[:, there].reshape(size, -1)
        for d in range(xs):
            @pl.when(lax.rem(aux + d, xs) == there)
            def _():
                outs[d][row : row + size, col : col + piece.shape[1]] = piece


def wide(refs, core=None):
    parts = []
    for ref in refs:
        for q in range(ref.shape[0]):
            part = ref[q] if core is None else ref[q, :, core]
            parts.append(part.reshape(-1, part.shape[-1]))
    return jnp.concatenate(parts, axis=1)


def split_kernel(place, kept, got, *outs):
    store_by_aux(place[2], kept[...] + got[...], outs, 0, 0)


def early_kernel(place, mine, mine2, above, above2, below, below2, *outs):
    core, aux = place[0], place[2]
    n = above.shape[1] * above.shape[2] * above.shape[3]
    own, up = wide((mine, mine2), core), wide((above, above2), core)
    store_by_aux(aux, times_transposed(own, wide((above, above2))), outs, 0, 0)
    both = times_transposed(jnp.concatenate([up, own], axis=0), wide((below, below2)))
    store_by_aux(aux, both[: up.shape[0]], outs, 0, n)
    store_by_aux(aux, both[up.shape[0] :], outs, 0, 2 * n)


def late_kernel(place, below, mine, above, across, *refs):
    given, *outs = refs
    core, aux = place[0], place[2]
    left = [wide((slab,), core) for slab in (below, mine, above)]
    product = times_transposed(jnp.concatenate(left, axis=0), wide((across,)))
    size = left[0].shape[0]
    outer, middle = outs[: len(outs) // 2], outs[len(outs) // 2 :]
    for at, (to, row) in enumerate(((outer, 0), (middle, 0), (outer, middle[0].shape[0]))):
        rows = slice(at * size, (at + 1) * size)
        store_by_aux(aux, product[rows] + given[rows, :], to, row, 0)


def own_kernel(place, below, mine, above, across, _, out):
    core = place[0]
    left = [wide((slab,), core) for slab in (below, mine, above)]
    out[...] = times_transposed(jnp.concatenate(left, axis=0), wide((across,)))


def pairs(kernel, place, operands, shapes, after=(), flops=1, limit=24 * MIB):
    return pl.pallas_call(
        kernel,
        in_specs=[SCALARS] + [ANYWHERE] * len(operands) + [AFTER] * len(after),
        out_specs=[ANYWHERE] * len(shapes),
        out_shape=[jax.ShapeDtypeStruct(shape, jnp.float32) for shape in shapes],
        compiler_params=pltpu.CompilerParams(vmem_limit_bytes=limit),
        cost_estimate=pl.CostEstimate(flops=flops, bytes_accessed=1, transcendentals=0),
        name=kernel.__name__,
    )(place, *operands, *after)


def spread_kernel(ys, place, rows, out):
    peers = out.shape[0] // ys
    n = rows.shape[1] // 7
    size = n // peers
    out[...] = jnp.zeros_like(out)
    for step in range(1, ys):
        first = lax.rem(place[1] + step, ys) * peers
        for k in range(peers):
            begin = (ys - 1 + step) * n + k * size
            out[first + k, :, :size] = rows[:, begin : begin + size]


def finish_kernel(ys, place, rows, pieces, out):
    peers = pieces.shape[0] // ys
    n = out.shape[1] // ys
    zs = n // peers // 8
    for step in range(ys):
        owner = lax.rem(place[1] + step, ys)
        block = rows[:, step * n : (step + 1) * n]
        if step:
            came = [pieces[owner * peers + k] for k in range(peers)]
            parts = [came[k][:, at * 8 : (at + 1) * 8] for at in range(zs) for k in range(peers)]
            block = block + jnp.concatenate(parts, axis=1)
        out[:, pl.ds(pl.multiple_of(owner * n, n), n)] = block


def small(kernel, shape, *operands):
    ys = 4
    return pl.pallas_call(
        functools.partial(kernel, ys),
        in_specs=[SCALARS] + [ANYWHERE] * (len(operands) - 1),
        out_specs=ANYWHERE,
        out_shape=jax.ShapeDtypeStruct(shape, jnp.float32),
        compiler_params=pltpu.CompilerParams(vmem_limit_bytes=4 * MIB),
        cost_estimate=pl.CostEstimate(flops=1, bytes_accessed=1, transcendentals=0),
        name=kernel.__name__,
    )(*operands)


def over_aux(parts, xs):
    there = {d: shift(parts[d], "aux", d, xs) for d in (2, 1, 3)}
    return [parts[0], there[2], there[3], there[1]]


def turn(block, zs):
    rows, cols = block.shape
    turned = block.T.reshape(zs, cols // zs // 8, 8, rows)
    return [[turned[at, k] for k in range(turned.shape[1])] for at in range(zs)]


def send_out(place, buffer, outs):
    zs, _, width = buffer.shape
    here, forward, backward, up, down = outs
    for out, step in ((here, 0), (forward, 3), (backward, 5)):
        out[...] = buffer[lax.rem(place[3] + step, zs)]
    for out, steps in ((up, (1, 6)), (down, (7, 2))):
        for at, step in enumerate(steps):
            out[:, at * width : (at + 1) * width] = buffer[lax.rem(place[3] + step, zs)]
    half = width // 2
    opposite = lax.rem(place[3] + zs // 2, zs)
    up[:, 2 * width :] = buffer[opposite, :, :half]
    down[:, 2 * width :] = buffer[opposite, :, half:]


def pack_kernel(place, *refs):
    diags, (early, third, middle, up, down), outs, buffer = refs[:4], refs[4:9], refs[9:-1], refs[-1]
    zs = buffer.shape[0]
    n = third.shape[1]
    buffer[:, :, :n] = (diags[0][...] + diags[1][...] + diags[2][...] + diags[3][...]).reshape(zs, 8, n)
    blocks = (early[:, :n] + up[...], third[...] + middle[...], early[:, 2 * n :] + down[...])
    for at, block in enumerate(blocks):
        buffer[:, :, (1 + at) * n : (2 + at) * n] = block.reshape(zs, 8, n)
        size = block.shape[0]
        for owner, pieces in enumerate(turn(block, zs)):
            for k, piece in enumerate(pieces):
                lane = (4 + at) * n + k * size
                buffer[owner, :, lane : lane + size] = piece
    send_out(place, buffer, outs)


def pack(place, *operands):
    zs = 8
    width = 7 * operands[0].shape[1]
    shapes = [(8, width)] * 3 + [(8, 2 * width + width // 2)] * 2
    return pl.pallas_call(
        pack_kernel,
        in_specs=[SCALARS] + [ANYWHERE] * len(operands),
        out_specs=[ANYWHERE] * len(shapes),
        out_shape=[jax.ShapeDtypeStruct(s, jnp.float32) for s in shapes],
        scratch_shapes=[pltpu.VMEM((zs, 8, width), jnp.float32)],
        compiler_params=pltpu.CompilerParams(vmem_limit_bytes=8 * MIB),
        cost_estimate=pl.CostEstimate(flops=1, bytes_accessed=1, transcendentals=0),
        name="pack",
    )(place, *operands)


def first_z(packed):
    zs = 8
    here, forward, backward, up, down = packed
    width = here.shape[1]
    half = width // 2
    up, down = shift(up, "z", 1, zs), shift(down, "z", -1, zs)
    here = here + up[:, :width] + down[:, :width]
    forward = forward + down[:, width : 2 * width]
    forward = jnp.concatenate([forward[:, :half] + up[:, 2 * width :], forward[:, half:]], axis=1)
    backward = backward + up[:, width : 2 * width]
    backward = jnp.concatenate([backward[:, :half], backward[:, half:] + down[:, 2 * width :]], axis=1)
    return here, forward, backward


def second_z(here, forward, backward):
    zs = 8
    return here, shift(forward, "z", 3, zs), shift(backward, "z", -3, zs)


def total_kernel(waits, *refs):
    parts, out = refs[: len(refs) - 1 - waits], refs[-1]
    value = parts[0][...]
    for part in parts[1:]:
        value = value + part[...]
    out[...] = value


def total(parts, after=(), flops=1):
    return pl.pallas_call(
        functools.partial(total_kernel, len(after)),
        in_specs=[ANYWHERE] * len(parts) + [AFTER] * len(after),
        out_specs=ANYWHERE,
        out_shape=jax.ShapeDtypeStruct(parts[0].shape, parts[0].dtype),
        compiler_params=pltpu.CompilerParams(vmem_limit_bytes=4 * MIB),
        cost_estimate=pl.CostEstimate(flops=flops, bytes_accessed=1, transcendentals=0),
        name="total",
    )(*parts, *after)


def body(half_transformed, screen):
    qrows, mrows, icols = half_transformed.shape
    ys, zs, xs = 4, 8, 4
    quarter = qrows // ys
    row, z = lax.axis_index("row"), lax.axis_index("z")
    core, aux = lax.axis_index("core"), lax.axis_index("aux")
    place = jnp.stack([core, row, aux, z]).astype(jnp.int32)
    n = mrows
    tiles = mrows // TILE
    local = lax.dynamic_slice(screen, (aux * qrows, row * tiles), (qrows, tiles))
    keep = jnp.repeat(local, TILE, axis=1).astype(jnp.bfloat16)

    def slab(block, step):
        first = lax.rem(row + step, ys) * quarter
        part = lax.dynamic_slice(block, (first, 0, 0), (quarter, mrows, icols))
        return part * lax.dynamic_slice(keep, (first, 0), (quarter, mrows))[:, :, None]

    to_up, to_down = slab(half_transformed, 1), slab(half_transformed, 3)
    block, to_up, to_down = lax.optimization_barrier((half_transformed, to_up, to_down))
    below = shift(to_up, "row", 1, ys)
    above = shift(to_down, "row", -1, ys)
    mine, far = slab(block, 0), slab(block, 2)
    mine2 = sibling(mine)
    kept, given = diagonal(place, screen, block, zs)
    diag = pairs(split_kernel, place, (kept, sibling(given)), [(zs * 8, n)] * xs, limit=4 * MIB)
    diag = over_aux(diag, xs)
    below, above, far, diag = lax.optimization_barrier((below, above, far, diag))
    across = shift(far, "row", 2, ys)

    def grouped(*slabs):
        return [s.reshape(quarter, zs, 2, n // zs // 2, icols) for s in slabs]

    mine, mine2 = grouped(mine, mine2)
    below, above = grouped(below, sibling(below)), grouped(above, sibling(above))
    early_parts = pairs(early_kernel, place, (mine, mine2, *above, *below), [(zs * 8, 3 * n)] * xs)
    early = total(over_aux(early_parts, xs), flops=SOME)
    third = shift(early[:, n : 2 * n], "row", 1, ys)
    (across_own,) = grouped(across)
    (across_sibling,) = grouped(sibling(across))
    (own,) = pairs(own_kernel, place, (below[0], mine, above[0], across_own), [(3 * n // 2, n)], (early,))
    shapes = [(2 * zs * 8, n)] * xs + [(zs * 8, n)] * xs
    late_parts = pairs(late_kernel, place, (below[1], mine2, above[1], across_sibling, own), shapes)
    outer = total(over_aux(late_parts[:xs], xs))
    middle = total(over_aux(late_parts[xs:], xs), (third,))
    up, down = shift(outer[zs * 8 :], "row", 1, ys), shift(outer[: zs * 8], "row", -1, ys)
    rows = first_z(pack(place, *diag, early, third, middle, up, down))
    here, forward, backward = second_z(*rows)
    rows = here + forward + backward
    peers = 2 * xs
    pieces = small(spread_kernel, (ys * peers, 8, 128), place, rows)
    pieces = lax.all_to_all(pieces, ("row", "core", "aux"), 0, 0, tiled=True)
    return small(finish_kernel, (8, ys * n), place, rows, pieces)


def solution(mesh):
    rows, cols, aux = mesh.devices.shape
    split = Mesh(mesh.devices.reshape(rows, cols // 2, 2, aux), ("row", "z", "core", "aux"))
    in_specs = (P("aux", "row", ("z", "core")), P())
    out_specs = P(("row", "z", "core", "aux"), None)
    return jax.shard_map(body, mesh=split, in_specs=in_specs, out_specs=out_specs, check_vma=False)
```
